32 devices in a mesh: fsdp: 2 (over x), ctx: 16 (over z, y, core).
Axes of the slice: x: 2, y: 2, z: 4, core: 2. Of those that a mesh axis runs over, the one named last changes fastest.
Arguments:
- tokens: bfloat16 [1024, 4, 768], P('ctx', 'fsdp'), may hold values from -6 to 6
- lengths: int32 [4], P('fsdp'), may hold values from 1 to 1024, as said below
- cotangent: bfloat16 [1024, 4, 768], P('ctx', 'fsdp'), may hold values from -6 to 6
- attend_weight: float32 [3, 768, 768], P(None, 'fsdp', 'ctx'), may hold values from -0.3125 to 0.3125
- attend_first: float32 [3, 768, 768], P(None, 'fsdp', 'ctx'), may hold values from -32 to 32
- attend_second: float32 [3, 768, 768], P(None, 'fsdp', 'ctx'), may hold values from 2.048 to 8.192
- output_weight: float32 [768, 768], P('fsdp', 'ctx'), may hold values from -0.875 to 0.875
- output_first: float32 [768, 768], P('fsdp', 'ctx'), may hold values from -6 to 6
- output_second: float32 [768, 768], P('fsdp', 'ctx'), may hold values from 0.04096 to 0.16384
- expand_weight: float32 [768, 3072], P('fsdp', 'ctx'), may hold values from -0.21875 to 0.21875
- expand_first: float32 [768, 3072], P('fsdp', 'ctx'), may hold values from -6 to 6
- expand_second: float32 [768, 3072], P('fsdp', 'ctx'), may hold values from 0.16384 to 0.65536
- contract_weight: float32 [3072, 768], P('fsdp', 'ctx'), may hold values from -0.109375 to 0.109375
- contract_first: float32 [3072, 768], P('fsdp', 'ctx'), may hold values from -16 to 16
- contract_second: float32 [3072, 768], P('fsdp', 'ctx'), may hold values from 0.65536 to 2.62144
- vector_params: float32 [9216], P('ctx'), may hold values from -0.6 to 1.45
- vector_first: float32 [9216], P('ctx'), may hold values from -32 to 32
- vector_second: float32 [9216], P('ctx'), may hold values from 2.048 to 8.192
Outputs:
- layer_out: bfloat16 [1024, 4, 768], P('ctx', 'fsdp')
- tokens_grad: float32 [1024, 4, 768], P('ctx', 'fsdp')
- new_attend: float32 [3, 768, 768], P(None, 'fsdp', 'ctx')
- new_attend_first: float32 [3, 768, 768], P(None, 'fsdp', 'ctx')
- new_attend_second: float32 [3, 768, 768], P(None, 'fsdp', 'ctx')
- new_output: float32 [768, 768], P('fsdp', 'ctx')
- new_output_first: float32 [768, 768], P('fsdp', 'ctx')
- new_output_second: float32 [768, 768], P('fsdp', 'ctx')
- new_expand: float32 [768, 3072], P('fsdp', 'ctx')
- new_expand_first: float32 [768, 3072], P('fsdp', 'ctx')
- new_expand_second: float32 [768, 3072], P('fsdp', 'ctx')
- new_contract: float32 [3072, 768], P('fsdp', 'ctx')
- new_contract_first: float32 [3072, 768], P('fsdp', 'ctx')
- new_contract_second: float32 [3072, 768], P('fsdp', 'ctx')
- new_vector: float32 [9216], P('ctx')
- new_vector_first: float32 [9216], P('ctx')
- new_vector_second: float32 [9216], P('ctx')
The draws below stay inside these ranges and needn't reach their ends.
Inputs may be any that keep to these rules, and one draw needn't show every extreme that they name: `lengths`: in each group of 2 consecutive sequences one, drawn from the seed, has all 1024 positions valid.
All inputs are finite; a program needn't handle non-finite values.
Results may differ from the reference program's by a relative error of at most 0.013.
The reference program's roundings to bfloat16 on the way count: a program that leaves them out, or rounds other values in their place, can miss the bound.
Values may be sent and summed in bfloat16 or wider, within the bound.
A program may use at most 192 MiB of HBM per device.

```python
import math
import jax
import jax.numpy as jnp
from jax import lax

D = 768
HEADS = 12
HEAD_DIM = 64
FF = 3072
BLK = 64
SEQ_DEV = 2
STEP = 10
LEN = 1024
SEQS = 4
NVEC = 9216
N_FSDP = 2
N_CTX = 16


def draw_lengths(key, part):
    key = jax.random.fold_in(key, 5)
    first_key, second_key = jax.random.split(key)
    chosen = jax.random.randint(first_key, (SEQS // SEQ_DEV,), 0, SEQ_DEV)
    others = jax.random.randint(second_key, (SEQS,), 1, LEN + 1)
    place = jnp.arange(SEQS, dtype=jnp.int32)
    full = place % SEQ_DEV == chosen[place // SEQ_DEV]
    return jnp.where(full, LEN, others).astype(jnp.int32)


def draw_vector_params(key, part):
    key = jax.random.fold_in(key, 9)
    base = jax.random.truncated_normal(key, -3.0, 3.0, (NVEC,), jnp.float32)
    place = jnp.arange(NVEC, dtype=jnp.int32)
    is_gain = (place >= 4 * D) & (place < 5 * D) | (place >= 6 * D) & (place < 7 * D)
    return jnp.where(is_gain, 1.0 + 0.15 * base, 0.2 * base).astype(jnp.float32)


def level_of(own_key, dims, cuts, low, high):
    loudness, own = 1.0, jax.random.fold_in(own_key, 6)
    for axis_at, parts in cuts:
        heights = jnp.exp(jax.random.uniform(jax.random.fold_in(own, axis_at), (parts,), jnp.float32, low / len(cuts), high / len(cuts)))
        loudness = loudness * jnp.repeat(heights, dims[axis_at] // parts).reshape([-1 if axis == axis_at else 1 for axis in range(len(dims))])
    return loudness


def gaussian(stream_key, dims, scale, most, cuts=(), kind=jnp.bfloat16):
    values = jax.random.normal(stream_key, dims, jnp.float32) * scale
    if len(cuts) > 0:
        values = level_of(stream_key, dims, cuts, -0.22, 0.18) * values
    return jnp.clip(values, min=-most, max=most).astype(kind)


def setup_inputs(seed: int = 0) -> dict:
    key_of = jax.random.split(jax.random.key(seed), 19)
    return {
        "tokens": gaussian(key_of[0], (LEN, SEQS, D), 1.0, 6.0, ((0, 16), (1, 2))),
        "lengths": draw_lengths(jax.random.fold_in(key_of[18], 71), 0),
        "cotangent": gaussian(key_of[2], (LEN, SEQS, D), 1.0, 6.0, ((0, 16), (1, 2))),
        "attend_weight": gaussian(key_of[3], (3, D, D), (D // 2) ** -0.5, 0.3125, ((1, 2), (2, 16)), jnp.float32),
        "attend_first": gaussian(key_of[4], (3, D, D), (0.077 * (BLK * N_CTX * SEQ_DEV * N_FSDP) ** 0.5), 32.0, ((1, 2), (2, 16)), jnp.float32),
        "attend_second": jnp.clip(jnp.exp(math.log(8.192) - 1.3862944 * jax.random.uniform(key_of[5], (3, D, D), jnp.float32) ** level_of(key_of[5], (3, D, D), ((1, 2), (2, 16)), -0.2, 0.2)), 2.048, 8.192),
        "output_weight": gaussian(key_of[6], (D, D), (D // 16) ** -0.5, 0.875, ((0, 2), (1, 16)), jnp.float32),
        "output_first": gaussian(key_of[7], (D, D), (0.011 * (BLK * N_CTX * SEQ_DEV * N_FSDP) ** 0.5), 6.0, ((0, 2), (1, 16)), jnp.float32),
        "output_second": jnp.clip(jnp.exp(math.log(0.16384) - 1.3862944 * jax.random.uniform(key_of[8], (D, D), jnp.float32) ** level_of(key_of[8], (D, D), ((0, 2), (1, 16)), -0.2, 0.2)), 0.04096, 0.16384),
        "expand_weight": gaussian(key_of[9], (D, FF), D ** -0.5, 0.21875, ((0, 2), (1, 16)), jnp.float32),
        "expand_first": gaussian(key_of[10], (D, FF), (0.022 * (BLK * N_CTX * SEQ_DEV * N_FSDP) ** 0.5), 6.0, ((0, 2), (1, 16)), jnp.float32),
        "expand_second": jnp.clip(jnp.exp(math.log(0.65536) - 1.3862944 * jax.random.uniform(key_of[11], (D, FF), jnp.float32) ** level_of(key_of[11], (D, FF), ((0, 2), (1, 16)), -0.2, 0.2)), 0.16384, 0.65536),
        "contract_weight": gaussian(key_of[12], (FF, D), FF ** -0.5, 0.109375, ((0, 2), (1, 16)), jnp.float32),
        "contract_first": gaussian(key_of[13], (FF, D), (0.044 * (BLK * N_CTX * SEQ_DEV * N_FSDP) ** 0.5), 16.0, ((0, 2), (1, 16)), jnp.float32),
        "contract_second": jnp.clip(jnp.exp(math.log(2.62144) - 1.3862944 * jax.random.uniform(key_of[14], (FF, D), jnp.float32) ** level_of(key_of[14], (FF, D), ((0, 2), (1, 16)), -0.2, 0.2)), 0.65536, 2.62144),
        "vector_params": draw_vector_params(jax.random.fold_in(key_of[18], 71), 0),
        "vector_first": gaussian(key_of[16], (NVEC,), (0.077 * (BLK * N_CTX * SEQ_DEV * N_FSDP) ** 0.5), 32.0, ((0, 16),), jnp.float32),
        "vector_second": jnp.clip(jnp.exp(math.log(8.192) - 1.3862944 * jax.random.uniform(key_of[17], (NVEC,), jnp.float32) ** level_of(key_of[17], (NVEC,), ((0, 16),), -0.2, 0.2)), 2.048, 8.192),
    }


NORM_EPSILON = 1e-06
MASK_FILL = -1e+30
BETA_ONE = 0.9
BETA_TWO = 0.999
ADAM_EPSILON = 1e-08
WEIGHT_DECAY = 0.01
RATE_ATTEND = 0.08
RATE_OUTPUT = 0.2
RATE_EXPAND = 0.05
RATE_CONTRACT = 0.025
RATE_VECTOR = 0.3

@jax.custom_vjp
def low(v):
    return lax.optimization_barrier(v.astype(jnp.bfloat16)).astype(jnp.float32)

@jax.custom_vjp
def low_back(v):
    return v

def low_keep(v):
    return (low(v), None)

def low_pass(kept, grad):
    return (grad,)

def back_keep(v):
    return (v, None)

def back_low(kept, grad):
    return (low(grad),)
low.defvjp(low_keep, low_pass)
low_back.defvjp(back_keep, back_low)

def layer_norm(values, gain, shift):
    centre = values - lax.optimization_barrier(jnp.mean(values, axis=-1, keepdims=True))
    spread = lax.optimization_barrier(jnp.mean(centre * centre, axis=-1, keepdims=True))
    return centre * lax.rsqrt(spread + NORM_EPSILON) * gain + shift

def product(left, right):
    return jnp.dot(left, right, precision=lax.Precision.HIGHEST)

def layer(params, inputs, seq_lengths):
    attend_w, output_w, expand_w, contract_w, vector = params
    seq_len, count, width = inputs.shape
    bias_query = vector[0:D]
    bias_value = vector[D:2 * D]
    bias_out = vector[2 * D:3 * D]
    bias_contract = vector[3 * D:4 * D]
    gain_one = vector[4 * D:5 * D]
    shift_one = vector[5 * D:6 * D]
    gain_two = vector[6 * D:7 * D]
    shift_two = vector[7 * D:8 * D]
    bias_expand = vector[8 * D:8 * D + FF]
    rows_in = inputs.reshape(seq_len * count, width)
    proj = jnp.einsum('td,cde->cte', rows_in, low(attend_w), precision=lax.Precision.HIGHEST)
    query = low_back(low(proj[0] + bias_query))
    keys = low_back(low(proj[1]))
    values = low_back(low(proj[2] + bias_value))
    valid = jnp.arange(seq_len, dtype=jnp.int32)[None, :] < seq_lengths.astype(jnp.int32)[:, None]
    scale = 1.0 / math.sqrt(HEAD_DIM)

    def split_heads(rows):
        return rows.reshape(seq_len, count, HEADS, HEAD_DIM).transpose(2, 0, 1, 3)

    def one_head(triple):
        head_query, head_key, head_value = triple
        scores = low_back(jnp.einsum('qsd,ksd->sqk', head_query, head_key, precision=lax.Precision.HIGHEST) * scale)
        masked = jnp.where(valid[:, None, :], scores, MASK_FILL)
        peak = lax.optimization_barrier(jnp.max(masked, axis=-1, keepdims=True))
        log_total = peak + jnp.log(lax.optimization_barrier(jnp.sum(jnp.exp(masked - peak), axis=-1, keepdims=True)))
        probs = jnp.exp(masked - log_total)
        return jnp.einsum('sqk,ksd->qsd', low(probs), head_value, precision=lax.Precision.HIGHEST)
    context = lax.map(jax.checkpoint(one_head), (split_heads(query), split_heads(keys), split_heads(values)))
    context = context.transpose(1, 2, 0, 3).reshape(seq_len * count, width)
    context = low_back(low(context))
    attn = low_back(product(context, low(output_w)) + bias_out)
    mixed = layer_norm(rows_in + attn, gain_one, shift_one)
    pre = low_back(product(low(mixed), low(expand_w)) + bias_expand)
    act = low(jax.nn.gelu(pre, approximate=False))
    ffn = low_back(product(act, low(contract_w)) + bias_contract)
    result = layer_norm(mixed + ffn, gain_two, shift_two)
    return result.reshape(seq_len, count, width)

def adam_step(weight, first, second, grad, rate, decay):
    new_first = BETA_ONE * first + (1.0 - BETA_ONE) * grad
    new_second = BETA_TWO * second + (1.0 - BETA_TWO) * grad * grad
    first_hat = new_first / (1.0 - BETA_ONE ** STEP)
    second_hat = new_second / (1.0 - BETA_TWO ** STEP)
    new_weight = weight - rate * (first_hat / (jnp.sqrt(second_hat) + ADAM_EPSILON) + decay * weight)
    return (new_weight, new_first, new_second)

def reference(tokens, lengths, cotangent, attend_weight, attend_first, attend_second, output_weight, output_first, output_second, expand_weight, expand_first, expand_second, contract_weight, contract_first, contract_second, vector_params, vector_first, vector_second):
    params = (attend_weight, output_weight, expand_weight, contract_weight, vector_params)
    inputs = tokens.astype(jnp.float32).reshape(LEN, N_FSDP, SEQ_DEV, D).transpose(1, 0, 2, 3)
    backs = cotangent.astype(jnp.float32).reshape(LEN, N_FSDP, SEQ_DEV, D).transpose(1, 0, 2, 3)
    groups_len = lengths.astype(jnp.int32).reshape(N_FSDP, SEQ_DEV)

    def advance(totals, batch):
        block_in, block_len, block_back = batch

        def apply(weights, values):
            return layer(weights, values, block_len)
        result, pullback = jax.vjp(apply, params, block_in)
        weight_grads, input_grads = pullback(block_back)
        return (jax.tree.map(jnp.add, totals, weight_grads), (result, input_grads))
    zeros = jax.tree.map(lambda item: jnp.zeros(item.shape, jnp.float32), params)
    totals, (results, input_grads) = lax.scan(advance, zeros, (inputs, groups_len, backs))
    layer_out = results.transpose(1, 0, 2, 3).reshape(LEN, SEQS, D).astype(jnp.bfloat16)
    tokens_grad = input_grads.transpose(1, 0, 2, 3).reshape(LEN, SEQS, D)
    attend_new = adam_step(attend_weight, attend_first, attend_second, totals[0], RATE_ATTEND, WEIGHT_DECAY)
    output_new = adam_step(output_weight, output_first, output_second, totals[1], RATE_OUTPUT, WEIGHT_DECAY)
    expand_new = adam_step(expand_weight, expand_first, expand_second, totals[2], RATE_EXPAND, WEIGHT_DECAY)
    contract_new = adam_step(contract_weight, contract_first, contract_second, totals[3], RATE_CONTRACT, WEIGHT_DECAY)
    vector_new = adam_step(vector_params, vector_first, vector_second, totals[4], RATE_VECTOR, 0.0)
    return (layer_out, tokens_grad, attend_new[0], attend_new[1], attend_new[2], output_new[0], output_new[1], output_new[2], expand_new[0], expand_new[1], expand_new[2], contract_new[0], contract_new[1], contract_new[2], vector_new[0], vector_new[1], vector_new[2])
```

```python
import functools
import math

import jax
import jax.numpy as jnp
from jax import lax
from jax.experimental import pallas as pl
from jax.experimental.pallas import tpu as pltpu
from jax.sharding import PartitionSpec as P

D = 768
HEADS = 12
HEAD_DIM = 64
FF = 3072
STEP = 10


NORM_EPSILON = 1e-06
MASK_FILL = -1e30
BETA_ONE = 0.9
BETA_TWO = 0.999
ADAM_EPSILON = 1e-08
WEIGHT_DECAY = 0.01
RATE_ATTEND = 0.08
RATE_OUTPUT = 0.2
RATE_EXPAND = 0.05
RATE_CONTRACT = 0.025
RATE_VECTOR = 0.3


def norm_parts(values, gain, shift):
    centre = values - jnp.mean(values, axis=-1, keepdims=True)
    spread = jnp.mean(centre * centre, axis=-1, keepdims=True)
    inverse = lax.rsqrt(spread + NORM_EPSILON)
    normed = centre * inverse
    return (normed * gain + shift, normed, inverse)


def norm_back(grad_out, normed, inverse, gain):
    scaled = grad_out * gain
    centred = scaled - jnp.mean(scaled, axis=-1, keepdims=True)
    return inverse * (centred - normed * jnp.mean(scaled * normed, axis=-1, keepdims=True))


def exact_gelu(values):
    return jax.nn.gelu(values, approximate=False)


def adam_step(weight, first, second, grad, rate, decay):
    new_first = BETA_ONE * first + (1.0 - BETA_ONE) * grad
    new_second = BETA_TWO * second + (1.0 - BETA_TWO) * grad * grad
    first_hat = new_first / (1.0 - BETA_ONE**STEP)
    second_hat = new_second / (1.0 - BETA_TWO**STEP)
    new_weight = weight - rate * (
        first_hat / (jnp.sqrt(second_hat) + ADAM_EPSILON) + decay * weight
    )
    return (new_weight, new_first, new_second)


MESH = pl.DeviceIdType.MESH
NZ, NY, NCORE = 4, 2, 2


def place():
    x = lax.axis_index("fsdp")
    c = lax.axis_index("ctx")
    return x, c // 4, (c // 2) % 2, c % 2


def device_at(x, z, y, core):
    return (x, z * 4 + y * 2 + core)


def greet(partners):
    barrier = pltpu.get_barrier_semaphore()
    for partner in partners:
        pl.semaphore_signal(barrier, inc=1, device_id=partner, device_id_type=MESH)
    pl.semaphore_wait(barrier, len(partners))


def partners_of(x, z, y, core, use_x):
    found = [device_at(x, lax.rem(z + j, NZ), y, core) for j in range(1, NZ)]
    found += [device_at(x, z, 1 - y, core), device_at(x, z, y, 1 - core)]
    if use_x:
        found.append(device_at(1 - x, z, y, core))
    return found


def gather_kernel(parts, use_x, own_ref, out_ref, local_sem, z_s, z_r, a_s, a_r, b_s, b_r, c_s, c_r):
    x, z, y, core = place()
    xi = x if use_x else 0
    xo = 1 - x if use_x else 0
    greet(partners_of(x, z, y, core, use_x))
    core_peer = device_at(x, z, y, 1 - core)

    def chunk(p, gx, gz, gy, gc):
        start, rows, _ = parts[p]
        return out_ref.at[gx, gz, gy, gc, pl.ds(start, rows)]

    def copy(src, dst, send, recv, device):
        return pltpu.make_async_remote_copy(
            src_ref=src, dst_ref=dst, send_sem=send, recv_sem=recv, device_id=device, device_id_type=MESH
        )

    sent = []

    def send(src, dst, send_sem, recv_sem, device):
        item = copy(src, dst, send_sem, recv_sem, device)
        item.start()
        sent.append(item)

    def landed(dst, send_sem, recv_sem):
        copy(dst, dst, send_sem, recv_sem, core_peer).wait_recv()

    local = pltpu.make_async_copy(own_ref, out_ref.at[xi, z, y, core], local_sem)
    local.start()
    axis = {"x": device_at(1 - x, z, y, core), "y": device_at(x, z, 1 - y, core)}

    def flipped(p, gz, first, second):
        order = parts[p][2]
        gx, gy = xi, y
        for flip, name in zip((first, second), order):
            if flip and name == "x":
                gx = xo
            if flip and name == "y":
                gy = 1 - y
        return gx, gz, gy

    def source(p, k):
        start, rows, _ = parts[p]
        if k == 0:
            return own_ref.at[pl.ds(start, rows)]
        return chunk(p, xi, lax.rem(z + k, NZ), y, core)

    for p, (start, rows, order) in enumerate(parts):
        for j in range(1, NZ):
            send(
                own_ref.at[pl.ds(start, rows)],
                chunk(p, xi, z, y, core),
                z_s.at[p, j - 1],
                z_r.at[p, NZ - j - 1],
                device_at(x, lax.rem(z + j, NZ), y, core),
            )

    def level_zero(p, k):
        order = parts[p][2]
        gz = lax.rem(z + k, NZ)
        here = chunk(p, xi, gz, y, core)
        if k > 0:
            landed(here, z_s.at[p, k - 1], z_r.at[p, k - 1])
        src = source(p, k)
        send(src, here, a_s.at[p, k], a_r.at[p, k], axis[order[0]])
        if len(order) > 1:
            send(src, here, b_s.at[p, k, 0], b_r.at[p, k, 0], axis[order[1]])
        send(src, here, c_s.at[p, k, 0], c_r.at[p, k, 0], core_peer)

    def level_one(p, k):
        order = parts[p][2]
        gz = lax.rem(z + k, NZ)
        here = chunk(p, *flipped(p, gz, True, False), core)
        landed(here, a_s.at[p, k], a_r.at[p, k])
        if len(order) > 1:
            send(here, here, b_s.at[p, k, 1], b_r.at[p, k, 1], axis[order[1]])
        send(here, here, c_s.at[p, k, 1], c_r.at[p, k, 1], core_peer)

    def level_two(p, k):
        if len(parts[p][2]) < 2:
            return
        gz = lax.rem(z + k, NZ)
        for first in range(2):
            here = chunk(p, *flipped(p, gz, first == 1, True), core)
            landed(here, b_s.at[p, k, first], b_r.at[p, k, first])
            send(here, here, c_s.at[p, k, 2 + first], c_r.at[p, k, 2 + first], core_peer)

    for step in range(NZ + 2):
        for level, work in enumerate((level_zero, level_one, level_two)):
            k = step - level
            if 0 <= k < NZ:
                for p in range(len(parts)):
                    work(p, k)
    for k in range(NZ):
        gz = lax.rem(z + k, NZ)
        for p, (start, rows, order) in enumerate(parts):
            for at in range(4 if len(order) > 1 else 2):
                here = chunk(p, *flipped(p, gz, at % 2 == 1, at >= 2), 1 - core)
                landed(here, c_s.at[p, k, at], c_r.at[p, k, at])
    for item in sent:
        item.wait_send()
    local.wait()


def gather_blocks(own, parts, use_x, collective_id):
    n = len(parts)
    dma = pltpu.SemaphoreType.DMA
    return pl.pallas_call(
        functools.partial(gather_kernel, parts, use_x),
        out_shape=jax.ShapeDtypeStruct((2 if use_x else 1, NZ, NY, NCORE) + own.shape, own.dtype),
        in_specs=[pl.BlockSpec(memory_space=pl.ANY)],
        out_specs=pl.BlockSpec(memory_space=pl.ANY),
        scratch_shapes=[dma]
        + [dma((n, 3))] * 2
        + [dma((n, NZ))] * 2
        + [dma((n, NZ, 2))] * 2
        + [dma((n, NZ, 4))] * 2,
        compiler_params=pltpu.CompilerParams(collective_id=collective_id, has_side_effects=True),
    )(own)


def scatter_kernel(parts, use_x, g_ref, out_ref, r0, *rest):
    n = len(parts)
    ra, rb, rz = rest[:n], rest[n : 2 * n], rest[2 * n : 3 * n]
    c_s, c_r, a_s, a_r, b_s, b_r, z_s, z_r = rest[3 * n :]
    x, z, y, core = place()
    nx = 2 if use_x else 1
    xi = x if use_x else 0
    xo = 1 - x if use_x else 0
    greet(partners_of(x, z, y, core, use_x))
    core_peer = device_at(x, z, y, 1 - core)
    axis = {"x": device_at(1 - x, z, y, core), "y": device_at(x, z, 1 - y, core)}
    sent = []

    def copy(src, dst, send_sem, recv_sem, device):
        return pltpu.make_async_remote_copy(
            src_ref=src, dst_ref=dst, send_sem=send_sem, recv_sem=recv_sem, device_id=device, device_id_type=MESH
        )

    def send(src, dst, send_sem, recv_sem, device):
        item = copy(src, dst, send_sem, recv_sem, device)
        item.start()
        sent.append(item)

    def landed(dst, send_sem, recv_sem):
        copy(dst, dst, send_sem, recv_sem, core_peer).wait_recv()

    def added(one, two):
        return (one.astype(jnp.float32) + two.astype(jnp.float32)).astype(jnp.bfloat16)

    def goal(k):
        return lax.rem(z + 1 + k, NZ)

    for k in range(NZ):
        for gx in range(nx):
            send(g_ref.at[gx, goal(k), :, 1 - core], r0.at[k, gx], c_s.at[k, gx], c_r.at[k, gx], core_peer)

    def level_zero(k):
        for gx in range(nx):
            landed(r0.at[k, gx], c_s.at[k, gx], c_r.at[k, gx])

        @pl.loop(0, nx * NY)
        def _(at):
            gx, gy = at // NY, at % NY
            r0[k, gx, gy] = added(r0[k, gx, gy], g_ref[gx, goal(k), gy, core])

        for p, (start, rows, order) in enumerate(parts):
            if order[0] == "x":
                src = r0.at[k, xo, :, pl.ds(start, rows)]
            else:
                src = r0.at[k, :, 1 - y, pl.ds(start, rows)]
            send(src, ra[p].at[k], a_s.at[p, k], a_r.at[p, k], axis[order[0]])

    def level_one(k):
        for p, (start, rows, order) in enumerate(parts):
            landed(ra[p].at[k], a_s.at[p, k], a_r.at[p, k])
            for other in range(ra[p].shape[1]):
                if order[0] == "x":
                    mine = r0[k, xi, other, pl.ds(start, rows)]
                else:
                    mine = r0[k, other, y, pl.ds(start, rows)]
                ra[p][k, other] = added(ra[p][k, other], mine)
            if len(order) > 1:
                away = 1 - y if order[1] == "y" else 1 - x
                send(ra[p].at[k, away], rb[p].at[k], b_s.at[p, k], b_r.at[p, k], axis[order[1]])
            else:
                last(p, k, ra[p].at[k, 0])

    def level_two(k):
        for p, (start, rows, order) in enumerate(parts):
            if len(order) > 1:
                landed(rb[p].at[k], b_s.at[p, k], b_r.at[p, k])
                mine = ra[p][k, y if order[1] == "y" else x]
                rb[p][k] = added(rb[p][k], mine)
                last(p, k, rb[p].at[k])

    def last(p, k, total):
        if k < NZ - 1:
            send(total, rz[p].at[k], z_s.at[p, k], z_r.at[p, k], device_at(x, goal(k), y, core))

    for step in range(NZ + 2):
        for level, work in enumerate((level_zero, level_one, level_two)):
            k = step - level
            if 0 <= k < NZ:
                work(k)
    for p, (start, rows, order) in enumerate(parts):
        for k in range(NZ - 1):
            landed(rz[p].at[k], z_s.at[p, k], z_r.at[p, k])
        total = (rb[p][NZ - 1] if len(order) > 1 else ra[p][NZ - 1, 0]).astype(jnp.float32)
        for k in range(NZ - 1):
            total = total + rz[p][k].astype(jnp.float32)
        out_ref[pl.ds(start, rows)] = total
    for item in sent:
        item.wait_send()


def scatter_blocks(blocks, parts, use_x, collective_id):
    n = len(parts)
    rows, width = blocks.shape[-2:]
    nx = blocks.shape[0]
    dma = pltpu.SemaphoreType.DMA
    low = jnp.bfloat16
    return pl.pallas_call(
        functools.partial(scatter_kernel, parts, use_x),
        out_shape=jax.ShapeDtypeStruct((rows, width), jnp.float32),
        in_specs=[pl.BlockSpec(memory_space=pltpu.VMEM)],
        out_specs=pl.BlockSpec(memory_space=pltpu.VMEM),
        scratch_shapes=[pltpu.VMEM((NZ, nx, NY, rows, width), low)]
        + [pltpu.VMEM((NZ, NY if part[2][0] == "x" else nx, part[1], width), low) for part in parts]
        + [pltpu.VMEM((NZ if len(part[2]) > 1 else 1, part[1], width), low) for part in parts]
        + [pltpu.VMEM((NZ - 1, part[1], width), low) for part in parts]
        + [dma((NZ, nx))] * 2
        + [dma((n, NZ))] * 4
        + [dma((n, NZ - 1))] * 2,
        compiler_params=pltpu.CompilerParams(
            collective_id=collective_id, has_side_effects=True, vmem_limit_bytes=48 * 1024 * 1024
        ),
    )(blocks)


def halves(rows):
    half = rows // 2
    return ((0, half, ("y", "x")), (half, half, ("x", "y")))


def halves_back(rows):
    half = rows // 2
    return ((0, half, ("x", "y")), (half, half, ("y", "x")))


def split_three(values):
    high = values.astype(jnp.bfloat16)
    rest = values - high.astype(jnp.float32)
    middle = rest.astype(jnp.bfloat16)
    lowest = (rest - middle.astype(jnp.float32)).astype(jnp.bfloat16)
    return jnp.stack([high, middle, lowest])


def in_rows(values, lead, rows, width):
    flat = values.reshape(lead + (-1,))
    pad = [(0, 0)] * len(lead) + [(0, rows * width - flat.shape[-1])]
    return jnp.pad(flat, pad).reshape(lead + (rows, width))


def on_device(
    tokens,
    lengths,
    cotangent,
    attend_weight,
    attend_first,
    attend_second,
    output_weight,
    output_first,
    output_second,
    expand_weight,
    expand_first,
    expand_second,
    contract_weight,
    contract_first,
    contract_second,
    vector_params,
    vector_first,
    vector_second,
):
    block, count, width = tokens.shape
    token_rows = block * count
    n_fsdp, n_ctx = lax.axis_size("fsdp"), lax.axis_size("ctx")
    own_topology = (n_fsdp, n_ctx) == (2, NZ * NY * NCORE)
    depth, wide = attend_weight.shape[1:]
    wide_ff = expand_weight.shape[1]
    folds = contract_weight.shape[0] // depth
    nvec = vector_params.shape[0]
    vec_rows = -(-3 * nvec // (depth * 32)) * 32
    mat_rows = 3 * wide + wide + wide_ff + folds * wide
    own = jnp.concatenate(
        [
            attend_weight.astype(jnp.bfloat16).transpose(0, 2, 1).reshape(3 * wide, depth),
            output_weight.astype(jnp.bfloat16).T,
            expand_weight.astype(jnp.bfloat16).T,
            contract_weight.astype(jnp.bfloat16)
            .reshape(folds, depth, wide)
            .transpose(0, 2, 1)
            .reshape(folds * wide, depth),
            in_rows(split_three(vector_params), (), vec_rows, depth),
        ]
    )
    if own_topology:
        gathered = gather_blocks(own, halves(own.shape[0]), True, 1)
    else:
        gathered = lax.all_gather(own, ("fsdp", "ctx"))
    gathered = gathered.reshape((n_fsdp, n_ctx) + own.shape)
    at = 3 * wide
    attend_back = (
        gathered[:, :, :at].reshape(n_fsdp, n_ctx, 3, wide, depth).transpose(2, 1, 3, 0, 4).reshape(3, D, D)
    )
    output_back = gathered[:, :, at : at + wide].transpose(1, 2, 0, 3).reshape(D, D)
    at += wide
    expand_back = gathered[:, :, at : at + wide_ff].transpose(1, 2, 0, 3).reshape(FF, D)
    at += wide_ff
    contract_back = (
        gathered[:, :, at : at + folds * wide]
        .reshape(n_fsdp, n_ctx, folds, wide, depth)
        .transpose(1, 3, 0, 2, 4)
        .reshape(D, FF)
    )
    thirds = gathered[0, :, mat_rows:].reshape(n_ctx, -1)[:, : 3 * nvec].reshape(n_ctx, 3, nvec)
    thirds = lax.optimization_barrier(thirds).astype(jnp.float32)
    vector = ((thirds[:, 0] + thirds[:, 1]) + thirds[:, 2]).reshape(-1)
    bias_query = vector[0:D]
    bias_value = vector[D : 2 * D]
    bias_out = vector[2 * D : 3 * D]
    bias_contract = vector[3 * D : 4 * D]
    gain_one = vector[4 * D : 5 * D]
    shift_one = vector[5 * D : 6 * D]
    gain_two = vector[6 * D : 7 * D]
    shift_two = vector[7 * D : 8 * D]
    bias_expand = vector[8 * D : 8 * D + FF]
    rows_in = tokens.reshape(token_rows, width)
    proj = jnp.einsum("td,ced->cte", rows_in, attend_back, preferred_element_type=jnp.float32)
    query = (proj[0] + bias_query).astype(jnp.bfloat16)
    local_keys = proj[1].astype(jnp.bfloat16).reshape(block, count, width)
    local_values = (proj[2] + bias_value).astype(jnp.bfloat16).reshape(block, count, width)
    if own_topology:
        both = jnp.stack([local_keys, local_values]).transpose(0, 2, 1, 3).reshape(2 * count * block, width)
        both = gather_blocks(both, ((0, 2 * count * block, ("y",)),), False, 2)
        both = both.reshape(n_ctx, 2, count, block, width)
        all_keys = both[:, 0].transpose(0, 2, 1, 3).reshape(n_ctx * block, count, width)
        all_values = both[:, 1].transpose(0, 2, 1, 3).reshape(n_ctx * block, count, width)
    else:
        all_keys = lax.all_gather(local_keys, "ctx", axis=0, tiled=True)
        all_values = lax.all_gather(local_values, "ctx", axis=0, tiled=True)
    seq_len = all_keys.shape[0]
    valid = (jnp.arange(seq_len, dtype=jnp.int32)[None, :] < lengths[:, None])[:, None, None, :]
    scale = 1.0 / math.sqrt(HEAD_DIM)
    head_query = query.reshape(block, count, HEADS, HEAD_DIM)

    def masked_scores(key_rows):
        key_heads = key_rows.reshape(seq_len, count, HEADS, HEAD_DIM)
        scores = (
            jnp.einsum("qshd,kshd->shqk", head_query, key_heads, preferred_element_type=jnp.float32)
            * scale
        )
        return jnp.where(valid, scores, MASK_FILL)

    masked = masked_scores(all_keys)
    peak = jnp.max(masked, axis=-1, keepdims=True)
    log_total = peak + jnp.log(jnp.sum(jnp.exp(masked - peak), axis=-1, keepdims=True))
    probs_low = jnp.exp(masked - log_total).astype(jnp.bfloat16)
    value_heads = all_values.reshape(seq_len, count, HEADS, HEAD_DIM)
    context = jnp.einsum(
        "shqk,kshd->qshd", probs_low, value_heads, preferred_element_type=jnp.float32
    )
    context = context.reshape(token_rows, width).astype(jnp.bfloat16)
    attn = jnp.einsum("te,de->td", context, output_back, preferred_element_type=jnp.float32) + bias_out
    mixed, normed_one, inverse_one = norm_parts(
        rows_in.astype(jnp.float32) + attn, gain_one, shift_one
    )
    mixed_low = mixed.astype(jnp.bfloat16)
    pre = jnp.einsum("td,fd->tf", mixed_low, expand_back, preferred_element_type=jnp.float32) + bias_expand
    act, gelu_back = jax.vjp(exact_gelu, pre)
    act_low = act.astype(jnp.bfloat16)
    ffn = jnp.einsum("tf,df->td", act_low, contract_back, preferred_element_type=jnp.float32) + bias_contract
    layer_out, normed_two, inverse_two = norm_parts(mixed + ffn, gain_two, shift_two)
    grad_out = cotangent.reshape(token_rows, width).astype(jnp.float32)
    grad_gain_two = jnp.sum(grad_out * normed_two, axis=0)
    grad_shift_two = jnp.sum(grad_out, axis=0)
    grad_resid = norm_back(grad_out, normed_two, inverse_two, gain_two)
    grad_ffn = grad_resid.astype(jnp.bfloat16)
    grad_bias_contract = jnp.sum(grad_ffn, axis=0, dtype=jnp.float32)
    grad_contract = jnp.einsum("tf,td->df", act_low, grad_ffn, preferred_element_type=jnp.float32)
    grad_act = jnp.einsum("td,df->tf", grad_ffn, contract_back, preferred_element_type=jnp.float32)
    grad_pre = gelu_back(grad_act)[0].astype(jnp.bfloat16)
    grad_bias_expand = jnp.sum(grad_pre, axis=0, dtype=jnp.float32)
    grad_expand = jnp.einsum("td,tf->fd", mixed_low, grad_pre, preferred_element_type=jnp.float32)
    grad_mixed = grad_resid + jnp.einsum(
        "tf,fd->td", grad_pre, expand_back, preferred_element_type=jnp.float32
    )
    grad_gain_one = jnp.sum(grad_mixed * normed_one, axis=0)
    grad_shift_one = jnp.sum(grad_mixed, axis=0)
    grad_attn = norm_back(grad_mixed, normed_one, inverse_one, gain_one)
    grad_attn_low = grad_attn.astype(jnp.bfloat16)
    grad_bias_out = jnp.sum(grad_attn_low, axis=0, dtype=jnp.float32)
    grad_output = jnp.einsum(
        "te,td->de", context, grad_attn_low, preferred_element_type=jnp.float32
    )
    grad_context = jnp.einsum(
        "td,de->te", grad_attn_low, output_back, preferred_element_type=jnp.float32
    ).astype(jnp.bfloat16)
    key_rows, value_rows = (all_keys, all_values)
    probs_full = jnp.exp(masked_scores(key_rows) - log_total)
    key_heads = key_rows.reshape(seq_len, count, HEADS, HEAD_DIM)
    value_back = value_rows.reshape(seq_len, count, HEADS, HEAD_DIM)
    context_heads = grad_context.reshape(block, count, HEADS, HEAD_DIM)
    grad_probs = jnp.einsum(
        "qshd,kshd->shqk", context_heads, value_back, preferred_element_type=jnp.float32
    )
    inner = jnp.sum(probs_full * grad_probs, axis=-1, keepdims=True)
    grad_scores = (probs_full * (grad_probs - inner)).astype(jnp.bfloat16)
    grad_query = (
        jnp.einsum("shqk,kshd->qshd", grad_scores, key_heads, preferred_element_type=jnp.float32)
        * scale
    )
    grad_query = grad_query.reshape(token_rows, width).astype(jnp.bfloat16)
    probs_back = probs_full.astype(jnp.bfloat16)
    size = lax.axis_size("ctx") * block
    grad_keys = (
        jnp.einsum("shqk,qshd->kshd", grad_scores, head_query, preferred_element_type=jnp.float32)
        * scale
    )
    grad_values = jnp.einsum(
        "shqk,qshd->kshd", probs_back, context_heads, preferred_element_type=jnp.float32
    )
    if own_topology:
        key_blocks = grad_keys.reshape(n_ctx, block, count, width).astype(jnp.bfloat16)
        value_blocks = grad_values.reshape(n_ctx, block, count, width).astype(jnp.bfloat16)
        blocks = jnp.stack([key_blocks, value_blocks], axis=1).transpose(0, 1, 3, 2, 4)
        rows = 2 * count * block
        summed = scatter_blocks(
            blocks.reshape(1, NZ, NY, NCORE, rows, width), ((0, rows, ("y",)),), False, 3
        )
        summed = summed.astype(jnp.bfloat16).reshape(2, count, block, width).transpose(0, 2, 1, 3)
        grad_keys_low = summed[0].reshape(token_rows, width)
        grad_values_low = summed[1].reshape(token_rows, width)
    else:
        summed = lax.psum_scatter(
            jnp.concatenate(
                [grad_keys.reshape(size, count, width), grad_values.reshape(size, count, width)], axis=2
            ),
            "ctx",
            scatter_dimension=0,
            tiled=True,
        )
        grad_keys_low = summed[:, :, :width].reshape(token_rows, width).astype(jnp.bfloat16)
        grad_values_low = summed[:, :, width:].reshape(token_rows, width).astype(jnp.bfloat16)
    stacked = jnp.stack([grad_query, grad_keys_low, grad_values_low])
    grad_attend = jnp.einsum("td,cte->ced", rows_in, stacked, preferred_element_type=jnp.float32)
    tokens_grad = grad_attn + jnp.einsum(
        "cte,ced->td", stacked, attend_back, preferred_element_type=jnp.float32
    )
    grad_vector = jnp.concatenate(
        [
            jnp.sum(grad_query, axis=0, dtype=jnp.float32),
            jnp.sum(grad_values_low, axis=0, dtype=jnp.float32),
            grad_bias_out,
            grad_bias_contract,
            grad_gain_one,
            grad_shift_one,
            grad_gain_two,
            grad_shift_two,
            grad_bias_expand,
        ]
    )
    if own_topology:
        cast = jnp.bfloat16
    else:
        cast = jnp.float32
    lead = (n_fsdp, n_ctx)
    vector_blocks = in_rows(grad_vector.astype(cast).reshape(n_ctx, nvec), (n_ctx,), vec_rows, depth)
    blocks = jnp.concatenate(
        [
            grad_attend.astype(cast)
            .reshape(3, n_ctx, wide, n_fsdp, depth)
            .transpose(3, 1, 0, 2, 4)
            .reshape(lead + (3 * wide, depth)),
            grad_output.astype(cast).reshape(n_ctx, wide, n_fsdp, depth).transpose(2, 0, 1, 3),
            grad_expand.astype(cast).reshape(n_ctx, wide_ff, n_fsdp, depth).transpose(2, 0, 1, 3),
            grad_contract.astype(cast)
            .reshape(n_ctx, wide, n_fsdp, folds, depth)
            .transpose(2, 0, 3, 1, 4)
            .reshape(lead + (folds * wide, depth)),
            jnp.broadcast_to(vector_blocks, lead + (vec_rows, depth)),
        ],
        axis=2,
    )
    if own_topology:
        total = scatter_blocks(
            blocks.reshape((2, NZ, NY, NCORE) + own.shape), halves_back(own.shape[0]), True, 4
        )
    else:
        total = lax.psum_scatter(
            blocks.reshape((n_fsdp * n_ctx,) + own.shape), ("fsdp", "ctx"), scatter_dimension=0, tiled=True
        ).reshape(own.shape)
    at = 3 * wide
    owned = (
        total[:at].reshape(3, wide, depth).transpose(0, 2, 1),
        total[at : at + wide].T,
        total[at + wide : at + wide + wide_ff].T,
        total[at + wide + wide_ff : mat_rows]
        .reshape(folds, wide, depth)
        .transpose(0, 2, 1)
        .reshape(folds * depth, wide),
    )
    vector_owned = total[mat_rows:].reshape(-1)[:nvec]
    attend_new = adam_step(
        attend_weight, attend_first, attend_second, owned[0], RATE_ATTEND, WEIGHT_DECAY
    )
    output_new = adam_step(
        output_weight, output_first, output_second, owned[1], RATE_OUTPUT, WEIGHT_DECAY
    )
    expand_new = adam_step(
        expand_weight, expand_first, expand_second, owned[2], RATE_EXPAND, WEIGHT_DECAY
    )
    contract_new = adam_step(
        contract_weight, contract_first, contract_second, owned[3], RATE_CONTRACT, WEIGHT_DECAY
    )
    vector_new = adam_step(
        vector_params, vector_first, vector_second, vector_owned, RATE_VECTOR, 0.0
    )
    return (
        layer_out.reshape(block, count, width).astype(jnp.bfloat16),
        tokens_grad.reshape(block, count, width),
        attend_new[0],
        attend_new[1],
        attend_new[2],
        output_new[0],
        output_new[1],
        output_new[2],
        expand_new[0],
        expand_new[1],
        expand_new[2],
        contract_new[0],
        contract_new[1],
        contract_new[2],
        vector_new[0],
        vector_new[1],
        vector_new[2],
    )


def solution(mesh):
    in_specs = (
        P("ctx", "fsdp", None),
        P("fsdp"),
        P("ctx", "fsdp", None),
        P(None, "fsdp", "ctx"),
        P(None, "fsdp", "ctx"),
        P(None, "fsdp", "ctx"),
        P("fsdp", "ctx"),
        P("fsdp", "ctx"),
        P("fsdp", "ctx"),
        P("fsdp", "ctx"),
        P("fsdp", "ctx"),
        P("fsdp", "ctx"),
        P("fsdp", "ctx"),
        P("fsdp", "ctx"),
        P("fsdp", "ctx"),
        P("ctx"),
        P("ctx"),
        P("ctx"),
    )
    out_specs = (
        P("ctx", "fsdp", None),
        P("ctx", "fsdp", None),
        P(None, "fsdp", "ctx"),
        P(None, "fsdp", "ctx"),
        P(None, "fsdp", "ctx"),
        P("fsdp", "ctx"),
        P("fsdp", "ctx"),
        P("fsdp", "ctx"),
        P("fsdp", "ctx"),
        P("fsdp", "ctx"),
        P("fsdp", "ctx"),
        P("fsdp", "ctx"),
        P("fsdp", "ctx"),
        P("fsdp", "ctx"),
        P("ctx"),
        P("ctx"),
        P("ctx"),
    )
    return jax.shard_map(
        on_device, mesh=mesh, in_specs=in_specs, out_specs=out_specs, check_vma=False
    )
```

```python
import functools
import math

import jax
import jax.numpy as jnp
from jax import lax
from jax.experimental import pallas as pl
from jax.experimental.pallas import tpu as pltpu
from jax.sharding import PartitionSpec as P

D = 768
HEADS = 12
HEAD_DIM = 64
FF = 3072
STEP = 10


NORM_EPSILON = 1e-06
MASK_FILL = -1e30
BETA_ONE = 0.9
BETA_TWO = 0.999
ADAM_EPSILON = 1e-08
WEIGHT_DECAY = 0.01
RATE_ATTEND = 0.08
RATE_OUTPUT = 0.2
RATE_EXPAND = 0.05
RATE_CONTRACT = 0.025
RATE_VECTOR = 0.3


def norm_parts(values, gain, shift):
    centre = values - jnp.mean(values, axis=-1, keepdims=True)
    spread = jnp.mean(centre * centre, axis=-1, keepdims=True)
    inverse = lax.rsqrt(spread + NORM_EPSILON)
    normed = centre * inverse
    return (normed * gain + shift, normed, inverse)


def norm_back(grad_out, normed, inverse, gain):
    scaled = grad_out * gain
    centred = scaled - jnp.mean(scaled, axis=-1, keepdims=True)
    return inverse * (centred - normed * jnp.mean(scaled * normed, axis=-1, keepdims=True))


def exact_gelu(values):
    return jax.nn.gelu(values, approximate=False)


def adam_step(weight, first, second, grad, rate, decay):
    new_first = BETA_ONE * first + (1.0 - BETA_ONE) * grad
    new_second = BETA_TWO * second + (1.0 - BETA_TWO) * grad * grad
    first_hat = new_first / (1.0 - BETA_ONE**STEP)
    second_hat = new_second / (1.0 - BETA_TWO**STEP)
    new_weight = weight - rate * (
        first_hat / (jnp.sqrt(second_hat) + ADAM_EPSILON) + decay * weight
    )
    return (new_weight, new_first, new_second)


MESH = pl.DeviceIdType.MESH
NZ, NY, NCORE = 4, 2, 2


def place():
    x = lax.axis_index("fsdp")
    c = lax.axis_index("ctx")
    return x, c // 4, (c // 2) % 2, c % 2


def device_at(x, z, y, core):
    return (x, z * 4 + y * 2 + core)


def greet(partners):
    barrier = pltpu.get_barrier_semaphore()
    for partner in partners:
        pl.semaphore_signal(barrier, inc=1, device_id=partner, device_id_type=MESH)
    pl.semaphore_wait(barrier, len(partners))


def partners_of(x, z, y, core, use_x):
    found = [device_at(x, lax.rem(z + j, NZ), y, core) for j in range(1, NZ)]
    found += [device_at(x, z, 1 - y, core), device_at(x, z, y, 1 - core)]
    if use_x:
        found.append(device_at(1 - x, z, y, core))
    return found


def remote(src, dst, send_sem, recv_sem, device):
    return pltpu.make_async_remote_copy(
        src_ref=src, dst_ref=dst, send_sem=send_sem, recv_sem=recv_sem, device_id=device, device_id_type=MESH
    )


def lanes(at, width):
    return pl.ds(pl.multiple_of(at * width, 128), width)


def gather_kernel(orders, use_x, *refs):
    n = len(orders)
    own_refs, out_refs = refs[:n], refs[n : 2 * n]
    local_sem, z_s, z_r, a_s, a_r, b_s, b_r, c_s, c_r = refs[2 * n :]
    x, z, y, core = place()
    greet(partners_of(x, z, y, core, use_x))
    core_peer = device_at(x, z, y, 1 - core)
    axis = {"x": device_at(1 - x, z, y, core), "y": device_at(x, z, 1 - y, core)}
    sent = []

    def chunk(p, gx, gz, gy, gc):
        out, c = out_refs[p], gz * 4 + gy * 2 + gc
        if not use_x:
            return out.at[c]
        half = lanes(gx, own_refs[p].shape[-1])
        return out.at[:, c, :, half] if len(out.shape) == 4 else out.at[c, :, half]

    def send(src, dst, send_sem, recv_sem, device):
        item = remote(src, dst, send_sem, recv_sem, device)
        item.start()
        sent.append(item)

    def landed(dst, send_sem, recv_sem):
        remote(dst, dst, send_sem, recv_sem, core_peer).wait_recv()

    def flipped(p, gz, first, second, gc):
        gx, gy = x, y
        for flip, name in zip((first, second), orders[p]):
            if flip and name == "x":
                gx = 1 - x
            if flip and name == "y":
                gy = 1 - y
        return chunk(p, gx, gz, gy, gc)

    local = [pltpu.make_async_copy(own_refs[p], chunk(p, x, z, y, core), local_sem.at[p]) for p in range(n)]
    for p in range(n):
        for j in range(1, NZ):
            there = device_at(x, lax.rem(z + j, NZ), y, core)
            send(own_refs[p], chunk(p, x, z, y, core), z_s.at[p, j - 1], z_r.at[p, NZ - j - 1], there)

    def level_zero(p, k):
        here = chunk(p, x, lax.rem(z + k, NZ), y, core)
        if k > 0:
            landed(here, z_s.at[p, k - 1], z_r.at[p, k - 1])
        src = here if k > 0 else own_refs[p]
        send(src, here, a_s.at[p, k], a_r.at[p, k], axis[orders[p][0]])
        if len(orders[p]) > 1:
            send(src, here, b_s.at[p, k, 0], b_r.at[p, k, 0], axis[orders[p][1]])
        send(src, here, c_s.at[p, k, 0], c_r.at[p, k, 0], core_peer)

    def level_one(p, k):
        here = flipped(p, lax.rem(z + k, NZ), True, False, core)
        landed(here, a_s.at[p, k], a_r.at[p, k])
        if len(orders[p]) > 1:
            send(here, here, b_s.at[p, k, 1], b_r.at[p, k, 1], axis[orders[p][1]])
        send(here, here, c_s.at[p, k, 1], c_r.at[p, k, 1], core_peer)

    def level_two(p, k):
        if len(orders[p]) < 2:
            return
        for first in range(2):
            here = flipped(p, lax.rem(z + k, NZ), first == 1, True, core)
            landed(here, b_s.at[p, k, first], b_r.at[p, k, first])
            send(here, here, c_s.at[p, k, 2 + first], c_r.at[p, k, 2 + first], core_peer)

    for step in range(NZ + 2):
        for level, work in enumerate((level_zero, level_one, level_two)):
            k = step - level
            if 0 <= k < NZ:
                for p in range(n):
                    work(p, k)
        if step == 0:
            for item in local:
                item.start()
    for k in range(NZ):
        for p in range(n):
            for at in range(4 if len(orders[p]) > 1 else 2):
                here = flipped(p, lax.rem(z + k, NZ), at % 2 == 1, at >= 2, 1 - core)
                landed(here, c_s.at[p, k, at], c_r.at[p, k, at])
    for item in sent:
        item.wait_send()
    for item in local:
        item.wait()


def gather_blocks(owns, orders, use_x, collective_id):
    n = len(orders)
    dma = pltpu.SemaphoreType.DMA
    count = NZ * NY * NCORE
    times = 2 if use_x else 1
    shapes = [o.shape[:-2] + (count, o.shape[-2], o.shape[-1] * times) for o in owns]
    anywhere = pl.BlockSpec(memory_space=pl.ANY)
    return pl.pallas_call(
        functools.partial(gather_kernel, orders, use_x),
        out_shape=[jax.ShapeDtypeStruct(s, o.dtype) for s, o in zip(shapes, owns)],
        in_specs=[anywhere] * n,
        out_specs=[anywhere] * n,
        scratch_shapes=[dma((n,))]
        + [dma((n, 3))] * 2
        + [dma((n, NZ))] * 2
        + [dma((n, NZ, 2))] * 2
        + [dma((n, NZ, 4))] * 2,
        compiler_params=pltpu.CompilerParams(collective_id=collective_id, has_side_effects=True),
    )(*owns)


def scatter_kernel(orders, use_x, *refs):
    n = len(orders)
    g, out = refs[:n], refs[n : 2 * n]
    r0, ra, rb, rz = (refs[i * n : (i + 1) * n] for i in range(2, 6))
    c_s, c_r, a_s, a_r, b_s, b_r, z_s, z_r = refs[6 * n :]
    x, z, y, core = place()
    greet(partners_of(x, z, y, core, use_x))
    core_peer = device_at(x, z, y, 1 - core)
    axis = {"x": device_at(1 - x, z, y, core), "y": device_at(x, z, 1 - y, core)}
    sent = []

    def send(src, dst, send_sem, recv_sem, device):
        item = remote(src, dst, send_sem, recv_sem, device)
        item.start()
        sent.append(item)

    def landed(dst, send_sem, recv_sem):
        remote(dst, dst, send_sem, recv_sem, core_peer).wait_recv()

    def added(one, two):
        return (one.astype(jnp.float32) + two.astype(jnp.float32)).astype(jnp.bfloat16)

    def goal(k):
        return lax.rem(z + 1 + k, NZ)

    def mine(p, k, gy, gc):
        c = goal(k) * 4 + gy * 2 + gc
        return g[p].at[:, c] if len(g[p].shape) == 4 else g[p].at[c]

    def half(p, gx):
        return lanes(gx, out[p].shape[-1])

    def columns(p, ref, gx):
        return ref.at[(slice(None),) * (len(ref.shape) - 1) + (half(p, gx),)]

    for k in range(NZ):
        for p in range(n):
            for gy in range(NY):
                send(mine(p, k, gy, 1 - core), r0[p].at[k, gy], c_s.at[p, k, gy], c_r.at[p, k, gy], core_peer)

    def level_zero(p, k):
        for gy in range(NY):
            landed(r0[p].at[k, gy], c_s.at[p, k, gy], c_r.at[p, k, gy])

        @pl.loop(0, NY)
        def _(gy):
            r0[p][k, gy] = added(r0[p][k, gy], mine(p, k, gy, core)[...])

        src = columns(p, r0[p].at[k], 1 - x) if orders[p][0] == "x" else r0[p].at[k, 1 - y]
        send(src, ra[p].at[k], a_s.at[p, k], a_r.at[p, k], axis[orders[p][0]])

    def level_one(p, k):
        landed(ra[p].at[k], a_s.at[p, k], a_r.at[p, k])
        kept = columns(p, r0[p].at[k], x) if orders[p][0] == "x" else r0[p].at[k, y]
        ra[p][k] = added(ra[p][k], kept[...])
        if len(orders[p]) > 1:
            src = columns(p, ra[p].at[k], 1 - x) if orders[p][1] == "x" else ra[p].at[k, 1 - y]
            send(src, rb[p].at[k], b_s.at[p, k], b_r.at[p, k], axis[orders[p][1]])
        else:
            last(p, k, ra[p].at[k])

    def level_two(p, k):
        if len(orders[p]) > 1:
            landed(rb[p].at[k], b_s.at[p, k], b_r.at[p, k])
            kept = columns(p, ra[p].at[k], x) if orders[p][1] == "x" else ra[p].at[k, y]
            rb[p][k] = added(rb[p][k], kept[...])
            last(p, k, rb[p].at[k])

    def last(p, k, total):
        if k < NZ - 1:
            send(total, rz[p].at[k], z_s.at[p, k], z_r.at[p, k], device_at(x, goal(k), y, core))

    for step in range(NZ + 2):
        for level, work in enumerate((level_zero, level_one, level_two)):
            k = step - level
            if 0 <= k < NZ:
                for p in range(n):
                    work(p, k)
    for p in range(n):
        for k in range(NZ - 1):
            landed(rz[p].at[k], z_s.at[p, k], z_r.at[p, k])
        total = (rb if len(orders[p]) > 1 else ra)[p][NZ - 1].astype(jnp.float32)
        for k in range(NZ - 1):
            total = total + rz[p][k].astype(jnp.float32)
        out[p][...] = total
    for item in sent:
        item.wait_send()


def scatter_blocks(blocks, orders, use_x, collective_id):
    n = len(orders)
    dma = pltpu.SemaphoreType.DMA
    times = 2 if use_x else 1
    fulls = [b.shape[:-3] + b.shape[-2:] for b in blocks]
    outs = [f[:-1] + (f[-1] // times,) for f in fulls]

    def buffers(shapes):
        return [pltpu.VMEM(s, jnp.bfloat16) for s in shapes]

    whole = pl.BlockSpec(memory_space=pltpu.VMEM)
    return pl.pallas_call(
        functools.partial(scatter_kernel, orders, use_x),
        out_shape=[jax.ShapeDtypeStruct(o, jnp.float32) for o in outs],
        in_specs=[whole] * n,
        out_specs=[whole] * n,
        scratch_shapes=buffers([(NZ, NY) + f for f in fulls])
        + buffers([(NZ, NY) + o if r[0] == "x" else (NZ,) + f for r, f, o in zip(orders, fulls, outs)])
        + buffers([((NZ if len(r) > 1 else 1),) + o for r, o in zip(orders, outs)])
        + buffers([(NZ - 1,) + o for o in outs])
        + [dma((n, NZ, NY))] * 2
        + [dma((n, NZ))] * 4
        + [dma((n, NZ - 1))] * 2,
        compiler_params=pltpu.CompilerParams(
            collective_id=collective_id, has_side_effects=True, vmem_limit_bytes=48 * 1024 * 1024
        ),
    )(*blocks)


PAIR = 2 * HEAD_DIM
SCALE = 1.0 / math.sqrt(HEAD_DIM)


def head_rows(rows):
    first = lax.broadcasted_iota(jnp.int32, rows.shape, 1) < HEAD_DIM
    zero = jnp.zeros_like(rows)
    return jnp.concatenate([jnp.where(first, rows, zero), jnp.where(first, zero, rows)])


def head_columns(both):
    block = both.shape[0] // 2
    first = lax.broadcasted_iota(jnp.int32, (block, PAIR), 1) < HEAD_DIM
    return jnp.where(first, both[:block], both[block:])


def along(one, two, dims):
    return lax.dot_general(one, two, ((dims[0], dims[1]), ((), ())), preferred_element_type=jnp.float32)


def pair_probs(length, query, keys):
    scores = along(query, keys, ((1,), (1,))) * SCALE
    at = lax.broadcasted_iota(jnp.int32, scores.shape, 1)
    masked = jnp.where(at < length, scores, MASK_FILL)
    peak = jnp.max(masked, axis=-1, keepdims=True)
    log_total = peak + jnp.log(jnp.sum(jnp.exp(masked - peak), axis=-1, keepdims=True))
    return jnp.exp(masked - log_total)


def pair_of(kv_ref):
    size = kv_ref.shape[0] * kv_ref.shape[3]
    return kv_ref[:, 0, 0].reshape(size, PAIR), kv_ref[:, 1, 0].reshape(size, PAIR)


def attend_kernel(len_ref, q_ref, kv_ref, out_ref):
    keys, values = pair_of(kv_ref)
    probs = pair_probs(len_ref[pl.program_id(0)], head_rows(q_ref[...]), keys)
    both = along(probs.astype(jnp.bfloat16), values, ((1,), (0,)))
    out_ref[...] = head_columns(both).astype(jnp.bfloat16)


def attend_back_kernel(len_ref, q_ref, kv_ref, grad_ref, dq_ref, dkv_ref):
    keys, values = pair_of(kv_ref)
    query, grad = head_rows(q_ref[...]), head_rows(grad_ref[...])
    probs = pair_probs(len_ref[pl.program_id(0)], query, keys)
    grad_probs = along(grad, values, ((1,), (1,)))
    inner = jnp.sum(probs * grad_probs, axis=-1, keepdims=True)
    grad_scores = (probs * (grad_probs - inner)).astype(jnp.bfloat16)
    dq_ref[...] = (head_columns(along(grad_scores, keys, ((1,), (0,)))) * SCALE).astype(jnp.bfloat16)
    shape = dkv_ref.shape[0], dkv_ref.shape[3], PAIR
    dkv_ref[:, 0, 0] = (along(grad_scores, query, ((0,), (0,))) * SCALE).reshape(shape).astype(dkv_ref.dtype)
    dkv_ref[:, 1, 0] = along(probs.astype(jnp.bfloat16), grad, ((0,), (0,))).reshape(shape).astype(dkv_ref.dtype)


def attend_call(lengths, query, kv, grad, low):
    count, block = kv.shape[2:4]
    rows = pl.BlockSpec((block, PAIR), lambda s, h: (s, h))
    kv_spec = pl.BlockSpec((kv.shape[0], 2, 1, block, PAIR), lambda s, h: (0, 0, s, 0, h))
    small = pl.BlockSpec(memory_space=pltpu.SMEM)
    rows_out = jax.ShapeDtypeStruct(query.shape, jnp.bfloat16)
    grid = (count, HEADS // 2)
    params = pltpu.CompilerParams(vmem_limit_bytes=48 * 1024 * 1024)
    if grad is None:
        return pl.pallas_call(
            attend_kernel,
            grid=grid,
            out_shape=rows_out,
            in_specs=[small, rows, kv_spec],
            out_specs=rows,
            compiler_params=params,
        )(lengths, query, kv)
    return pl.pallas_call(
        attend_back_kernel,
        grid=grid,
        out_shape=[rows_out, jax.ShapeDtypeStruct(kv.shape, low)],
        in_specs=[small, rows, kv_spec, rows],
        out_specs=[rows, kv_spec],
        compiler_params=params,
    )(lengths, query, kv, grad)


ORDERS = (("x", "y"), ("y", "x"), ("y", "x"), ("x", "y"), ("y", "x"))
ORDERS_BACK = tuple(order[::-1] for order in ORDERS)


def split_three(values):
    high = values.astype(jnp.bfloat16)
    rest = values - high.astype(jnp.float32)
    middle = rest.astype(jnp.bfloat16)
    lowest = (rest - middle.astype(jnp.float32)).astype(jnp.bfloat16)
    return jnp.stack([high, middle, lowest])


def in_rows(values, lead, rows, width):
    flat = values.reshape(lead + (-1,))
    pad = [(0, 0)] * len(lead) + [(0, rows * width - flat.shape[-1])]
    return jnp.pad(flat, pad).reshape(lead + (rows, width))


def on_device(
    tokens,
    lengths,
    cotangent,
    attend_weight,
    attend_first,
    attend_second,
    output_weight,
    output_first,
    output_second,
    expand_weight,
    expand_first,
    expand_second,
    contract_weight,
    contract_first,
    contract_second,
    vector_params,
    vector_first,
    vector_second,
):
    block, count, width = tokens.shape
    token_rows = block * count
    n_fsdp, n_ctx = lax.axis_size("fsdp"), lax.axis_size("ctx")
    own_topology = (n_fsdp, n_ctx) == (2, NZ * NY * NCORE)
    low = jnp.bfloat16 if own_topology else jnp.float32
    depth, wide = attend_weight.shape[1:]
    nvec = vector_params.shape[0]
    vec_rows = -(-3 * nvec // (depth * 32)) * 32
    owns = [
        attend_weight.astype(jnp.bfloat16).transpose(0, 2, 1),
        output_weight.astype(jnp.bfloat16).T,
        expand_weight.astype(jnp.bfloat16).T,
        contract_weight.astype(jnp.bfloat16).T,
        in_rows(split_three(vector_params), (), vec_rows, depth),
    ]
    if own_topology:
        fulls = gather_blocks(owns, ORDERS, True, 1)
    else:
        fulls = []
        for own in owns:
            wider = lax.all_gather(own, "fsdp", axis=own.ndim - 1, tiled=True)
            fulls.append(lax.all_gather(wider, "ctx", axis=own.ndim - 2))
    attend_back = fulls[0].reshape(3, D, D)
    output_back = fulls[1].reshape(D, D)
    expand_back = fulls[2].reshape(FF, D)
    contract_back = fulls[3].reshape(D, FF)
    thirds = fulls[4][:, :, :depth].reshape(n_ctx, -1)[:, : 3 * nvec].reshape(n_ctx, 3, nvec)
    thirds = lax.optimization_barrier(thirds).astype(jnp.float32)
    vector = ((thirds[:, 0] + thirds[:, 1]) + thirds[:, 2]).reshape(-1)
    bias_query = vector[0:D]
    bias_value = vector[D : 2 * D]
    bias_out = vector[2 * D : 3 * D]
    bias_contract = vector[3 * D : 4 * D]
    gain_one = vector[4 * D : 5 * D]
    shift_one = vector[5 * D : 6 * D]
    gain_two = vector[6 * D : 7 * D]
    shift_two = vector[7 * D : 8 * D]
    bias_expand = vector[8 * D : 8 * D + FF]
    rows_in = tokens.transpose(1, 0, 2).reshape(token_rows, width)
    proj = jnp.einsum("td,ced->cte", rows_in, attend_back, preferred_element_type=jnp.float32)
    query = (proj[0] + bias_query).astype(jnp.bfloat16)
    keys_values = jnp.stack([proj[1], proj[2] + bias_value]).astype(jnp.bfloat16).reshape(2 * token_rows, width)
    if own_topology:
        (kv,) = gather_blocks([keys_values], (("y",),), False, 2)
    else:
        kv = lax.all_gather(keys_values, "ctx")
    kv = kv.reshape(n_ctx, 2, count, block, width)
    context = attend_call(lengths, query, kv, None, low)
    attn = jnp.einsum("te,de->td", context, output_back, preferred_element_type=jnp.float32) + bias_out
    mixed, normed_one, inverse_one = norm_parts(
        rows_in.astype(jnp.float32) + attn, gain_one, shift_one
    )
    mixed_low = mixed.astype(jnp.bfloat16)
    pre = jnp.einsum("td,fd->tf", mixed_low, expand_back, preferred_element_type=jnp.float32) + bias_expand
    act, gelu_back = jax.vjp(exact_gelu, pre)
    act_low = act.astype(jnp.bfloat16)
    ffn = jnp.einsum("tf,df->td", act_low, contract_back, preferred_element_type=jnp.float32) + bias_contract
    layer_out, normed_two, inverse_two = norm_parts(mixed + ffn, gain_two, shift_two)
    grad_out = cotangent.transpose(1, 0, 2).reshape(token_rows, width).astype(jnp.float32)
    grad_gain_two = jnp.sum(grad_out * normed_two, axis=0)
    grad_shift_two = jnp.sum(grad_out, axis=0)
    grad_resid = norm_back(grad_out, normed_two, inverse_two, gain_two)
    grad_ffn = grad_resid.astype(jnp.bfloat16)
    grad_bias_contract = jnp.sum(grad_ffn, axis=0, dtype=jnp.float32)
    grad_contract = jnp.einsum("tf,td->df", act_low, grad_ffn, preferred_element_type=jnp.float32)
    grad_act = jnp.einsum("td,df->tf", grad_ffn, contract_back, preferred_element_type=jnp.float32)
    grad_pre = gelu_back(grad_act)[0].astype(jnp.bfloat16)
    grad_bias_expand = jnp.sum(grad_pre, axis=0, dtype=jnp.float32)
    grad_expand = jnp.einsum("td,tf->fd", mixed_low, grad_pre, preferred_element_type=jnp.float32)
    grad_mixed = grad_resid + jnp.einsum(
        "tf,fd->td", grad_pre, expand_back, preferred_element_type=jnp.float32
    )
    grad_gain_one = jnp.sum(grad_mixed * normed_one, axis=0)
    grad_shift_one = jnp.sum(grad_mixed, axis=0)
    grad_attn = norm_back(grad_mixed, normed_one, inverse_one, gain_one)
    grad_attn_low = grad_attn.astype(jnp.bfloat16)
    grad_bias_out = jnp.sum(grad_attn_low, axis=0, dtype=jnp.float32)
    grad_output = jnp.einsum(
        "te,td->de", context, grad_attn_low, preferred_element_type=jnp.float32
    )
    grad_context = jnp.einsum(
        "td,de->te", grad_attn_low, output_back, preferred_element_type=jnp.float32
    ).astype(jnp.bfloat16)
    grad_query, grad_kv = attend_call(lengths, query, kv, grad_context, low)
    grad_kv = grad_kv.reshape(n_ctx, 2 * token_rows, width)
    if own_topology:
        (summed,) = scatter_blocks([grad_kv], (("y",),), False, 3)
    else:
        summed = lax.psum_scatter(grad_kv, "ctx", scatter_dimension=0)
    grad_keys_low, grad_values_low = summed.astype(jnp.bfloat16).reshape(2, token_rows, width)
    stacked = jnp.stack([grad_query, grad_keys_low, grad_values_low])
    grad_attend = jnp.einsum("td,cte->ced", rows_in, stacked, preferred_element_type=jnp.float32)
    tokens_grad = grad_attn + jnp.einsum(
        "cte,ced->td", stacked, attend_back, preferred_element_type=jnp.float32
    )
    grad_vector = jnp.concatenate(
        [
            jnp.sum(grad_query, axis=0, dtype=jnp.float32),
            jnp.sum(grad_values_low, axis=0, dtype=jnp.float32),
            grad_bias_out,
            grad_bias_contract,
            grad_gain_one,
            grad_shift_one,
            grad_gain_two,
            grad_shift_two,
            grad_bias_expand,
        ]
    )
    vector_blocks = in_rows(grad_vector.reshape(n_ctx, nvec), (n_ctx,), vec_rows, depth)
    blocks = [
        grad_attend.astype(low).reshape(3, n_ctx, wide, D),
        grad_output.astype(low).reshape(n_ctx, wide, D),
        grad_expand.astype(low).reshape(n_ctx, FF // n_ctx, D),
        grad_contract.astype(low).reshape(n_ctx, wide, FF),
        jnp.concatenate([vector_blocks.astype(low)] * n_fsdp, axis=2),
    ]
    if own_topology:
        owned = scatter_blocks(blocks, ORDERS_BACK, True, 4)
    else:
        owned = []
        for item in blocks:
            part = lax.psum_scatter(item, "ctx", scatter_dimension=item.ndim - 3)
            owned.append(lax.psum_scatter(part, "fsdp", scatter_dimension=part.ndim - 1, tiled=True))
    vector_owned = owned[4].reshape(-1)[:nvec]
    owned = [jnp.swapaxes(item, -1, -2) for item in owned[:4]]
    attend_new = adam_step(
        attend_weight, attend_first, attend_second, owned[0], RATE_ATTEND, WEIGHT_DECAY
    )
    output_new = adam_step(
        output_weight, output_first, output_second, owned[1], RATE_OUTPUT, WEIGHT_DECAY
    )
    expand_new = adam_step(
        expand_weight, expand_first, expand_second, owned[2], RATE_EXPAND, WEIGHT_DECAY
    )
    contract_new = adam_step(
        contract_weight, contract_first, contract_second, owned[3], RATE_CONTRACT, WEIGHT_DECAY
    )
    vector_new = adam_step(
        vector_params, vector_first, vector_second, vector_owned, RATE_VECTOR, 0.0
    )
    return (
        layer_out.astype(jnp.bfloat16).reshape(count, block, width).transpose(1, 0, 2),
        tokens_grad.reshape(count, block, width).transpose(1, 0, 2),
        attend_new[0],
        attend_new[1],
        attend_new[2],
        output_new[0],
        output_new[1],
        output_new[2],
        expand_new[0],
        expand_new[1],
        expand_new[2],
        contract_new[0],
        contract_new[1],
        contract_new[2],
        vector_new[0],
        vector_new[1],
        vector_new[2],
    )


def solution(mesh):
    in_specs = (
        P("ctx", "fsdp", None),
        P("fsdp"),
        P("ctx", "fsdp", None),
        P(None, "fsdp", "ctx"),
        P(None, "fsdp", "ctx"),
        P(None, "fsdp", "ctx"),
        P("fsdp", "ctx"),
        P("fsdp", "ctx"),
        P("fsdp", "ctx"),
        P("fsdp", "ctx"),
        P("fsdp", "ctx"),
        P("fsdp", "ctx"),
        P("fsdp", "ctx"),
        P("fsdp", "ctx"),
        P("fsdp", "ctx"),
        P("ctx"),
        P("ctx"),
        P("ctx"),
    )
    out_specs = (
        P("ctx", "fsdp", None),
        P("ctx", "fsdp", None),
        P(None, "fsdp", "ctx"),
        P(None, "fsdp", "ctx"),
        P(None, "fsdp", "ctx"),
        P("fsdp", "ctx"),
        P("fsdp", "ctx"),
        P("fsdp", "ctx"),
        P("fsdp", "ctx"),
        P("fsdp", "ctx"),
        P("fsdp", "ctx"),
        P("fsdp", "ctx"),
        P("fsdp", "ctx"),
        P("fsdp", "ctx"),
        P("ctx"),
        P("ctx"),
        P("ctx"),
    )
    return jax.shard_map(
        on_device, mesh=mesh, in_specs=in_specs, out_specs=out_specs, check_vma=False
    )
```
